32 devices in a mesh: groups: 2 (over x), tensor: 16 (over z, y, core).
Axes of the slice: x: 2, y: 2, z: 4, core: 2. Of those that a mesh axis runs over, the one named last changes fastest.
Arguments:
- tokens: bfloat16 [256, 8192], P(('groups', 'tensor')), parts along dimension 0, may hold values from -6 to 6
- adapter_ids: int32 [256], P(('groups', 'tensor')), parts along dimension 0, may hold values from 0 to 15, as said below
- gate_weight: bfloat16 [8192, 16384], P(None, 'tensor'), may hold values from -0.0625 to 0.0625
- up_weight: bfloat16 [8192, 16384], P(None, 'tensor'), may hold values from -0.0625 to 0.0625
- shrink_factors: bfloat16 [16, 8192, 64], P('tensor'), may hold values from -0.0625 to 0.0625
- expand_factors: bfloat16 [16, 64, 16384], P(None, None, 'tensor'), may hold values from -0.75 to 0.75
Outputs:
- hidden: bfloat16 [256, 16384], P('groups', 'tensor'), parts along dimension 0
The draws below stay inside these ranges and needn't reach their ends.
There are 2 independent parts, one for each index of `groups`. The reference program is written for one: setup_inputs(seed, part) draws one part's arguments, and reference() takes and returns one part's arrays. A program takes and returns all parts, laid end to end along the dimension named above; an argument that names none is the same for every part. Nothing has to cross between parts.
Inputs may be any that keep to these rules, and one draw needn't show every extreme that they name: `adapter_ids`: no adapter is named by more than 32 rows of a group, and one adapter by exactly 32.
All inputs are finite; a program needn't handle non-finite values.
Results may differ from the reference program's by a relative error of at most 0.0037.
Values may be sent and summed in bfloat16 or wider, within the bound.
A program may use at most 128 MiB of HBM per device.

```python
import jax
import jax.numpy as jnp
from jax import lax

D = 8192
FF = 16384
RANK = 64
ROWS_DEV = 8
ROWS = 128
ADAPTERS = 16


def draw_adapter_ids(key, part):
    key = jax.random.fold_in(key, 11)
    key_hot, key_jitter, key_order, key_shuffle = jax.random.split(key, 4)
    hot_count = 4 * ROWS_DEV
    other_count = ROWS - hot_count
    hot_adapter = jax.random.randint(key_hot, (), 0, ADAPTERS)
    jitter = jax.random.randint(key_jitter, (other_count,), 0, 2)
    order = jax.random.permutation(key_order, ADAPTERS - 1)
    slot = (jnp.arange(other_count) + jitter) % (ADAPTERS - 1)
    others = (hot_adapter + 1 + order[slot]) % ADAPTERS
    pool = jnp.concatenate([jnp.full((hot_count,), hot_adapter, jnp.int32), others.astype(jnp.int32)])
    return jax.random.permutation(key_shuffle, pool).astype(jnp.int32)


def block_levels(stream_key, dims, shards, low, largest):
    loudness = 1.0
    for position, parts in shards:
        steps = jax.random.uniform(jax.random.fold_in(jax.random.fold_in(stream_key, 6), position), (parts,), jnp.float32, low / len(shards), largest / len(shards))
        loudness = loudness * jnp.repeat(jnp.exp(steps), dims[position] // parts).reshape((-1,) + (1,) * (len(dims) - 1 - position))
    return loudness


def normal_values(stream_key, dims, width, bound, cuts=(), dtype=jnp.bfloat16):
    factor_of = block_levels(stream_key, dims, cuts, -0.22, 0.18) if cuts else 1.0
    result = jax.random.normal(stream_key, dims, jnp.float32) * width * factor_of
    return jnp.minimum(jnp.maximum(result, -bound), bound).astype(dtype)


def setup_inputs(seed: int = 0, part: int = 0) -> dict:
    streams_of = jax.random.split(jax.random.key(seed), 7)
    part_splits = jax.random.split(jax.random.fold_in(streams_of[6], part), 7)
    return {
        "tokens": normal_values(part_splits[0], (ROWS, D), 1.0, 6.0, ((0, 16),)),
        "adapter_ids": draw_adapter_ids(jax.random.fold_in(jax.random.fold_in(streams_of[6], part), 71), part),
        "gate_weight": normal_values(streams_of[2], (D, FF), D ** -0.5, 0.0625, ((1, 16),)),
        "up_weight": normal_values(streams_of[3], (D, FF), D ** -0.5, 0.0625, ((1, 16),)),
        "shrink_factors": normal_values(streams_of[4], (ADAPTERS, D, RANK), D ** -0.5, 0.0625, ((0, 16),)),
        "expand_factors": normal_values(streams_of[5], (ADAPTERS, RANK, FF), RANK ** -0.5, 0.75, ((2, 16),)),
    }


def reference(tokens, adapter_ids, gate_weight, up_weight, shrink_factors, expand_factors):
    gate_sum = jnp.dot(tokens, gate_weight, preferred_element_type=jnp.float32)
    up_sum = jnp.dot(tokens, up_weight, preferred_element_type=jnp.float32)
    blocks = ROWS // 32
    row_blocks = tokens.reshape(blocks, 32, D)
    id_blocks = adapter_ids.reshape(blocks, 32)

    def shrink_block(block_item):
        piece_rows, piece_ids = block_item
        picked = jnp.take(shrink_factors, piece_ids, axis=0).astype(jnp.float32)
        return jnp.einsum("rd,rdk->rk", piece_rows.astype(jnp.float32), picked)

    shrunk = lax.map(shrink_block, (row_blocks, id_blocks)).reshape(ROWS, RANK).astype(jnp.bfloat16)

    def expand_block(block_item):
        piece_low, piece_ids = block_item
        picked = jnp.take(expand_factors, piece_ids, axis=0).astype(jnp.float32)
        return jnp.einsum("rk,rkf->rf", piece_low.astype(jnp.float32), picked)

    delta_up = lax.map(expand_block, (shrunk.reshape(blocks, 32, RANK), id_blocks)).reshape(ROWS, FF)
    return (jax.nn.silu(gate_sum) * (up_sum + delta_up)).astype(jnp.bfloat16)
```

```python
import functools

import jax
import jax.numpy as jnp
from jax import lax
from jax.experimental import pallas as pl
from jax.experimental.pallas import tpu as pltpu
from jax.sharding import PartitionSpec as P

CORES = 2
LAG = 2


def each(count, body):
    if count <= 4:
        for i in range(count):
            body(i)
    else:
        lax.fori_loop(0, count, lambda i, carry: (body(i), carry)[1], 0)


def step_kernel(
    line, pairs, pieces,
    tokens, ids, gate_weight, up_weight, shrink, expand,
    out,
    rows_in, gate_in, up_in, shrink_in, expand_in, left, gate_acc, up_acc, shrink_acc,
    id_rows, packed, slots_of, wide,
    own_sem, gate_sem, up_sem, small_sem, z_send, z_recv, y_send, y_recv, c_send, c_recv,
    id_send, id_recv, p_send, p_recv,
):
    total = line * pairs * CORES
    row_dev = tokens.shape[0]
    rows = total * row_dev
    depth = tokens.shape[1] // pieces
    rank = shrink.shape[1]
    half = packed.shape[1]
    adapters = expand.shape[0] // rank

    me = lax.axis_index("tensor")
    k = lax.rem(me, CORES)
    y = lax.rem(me // CORES, pairs)
    z = me // (CORES * pairs)

    def place(zz, yy, kk):
        return {"tensor": (zz * pairs + yy) * CORES + kk}

    def peer(i):
        return {"tensor": lax.rem(me + 1 + i, total)}

    def own_copy(c):
        return pltpu.make_async_copy(
            tokens.at[:, pl.ds(c * depth, depth)], rows_in.at[c, k, y, z], own_sem.at[c]
        )

    def gate_copy(c):
        where = pl.ds(pl.multiple_of(c * depth, depth), depth)
        return pltpu.make_async_copy(gate_weight.at[where], gate_in.at[where], gate_sem.at[c])

    def up_copy(c):
        where = pl.ds(pl.multiple_of(c * depth, depth), depth)
        return pltpu.make_async_copy(up_weight.at[where], up_in.at[where], up_sem.at[c])

    shrink_copy = pltpu.make_async_copy(shrink, shrink_in, small_sem.at[0])
    expand_copy = pltpu.make_async_copy(expand, expand_in, small_sem.at[1])

    def z_copy(c, d):
        block = rows_in.at[c, k, y, z]
        return pltpu.make_async_remote_copy(
            block, block, z_send.at[c, d], z_recv.at[c, d],
            device_id=place(lax.rem(z + d + 1, line), y, k), device_id_type=pl.DeviceIdType.MESH,
        )

    def y_copy(c):
        block = rows_in.at[c, k, y]
        return pltpu.make_async_remote_copy(
            block, block, y_send.at[c], y_recv.at[c],
            device_id=place(z, 1 - y, k), device_id_type=pl.DeviceIdType.MESH,
        )

    def c_copy(c):
        block = rows_in.at[c, k]
        return pltpu.make_async_remote_copy(
            block, block, c_send.at[c], c_recv.at[c],
            device_id=place(z, y, 1 - k), device_id_type=pl.DeviceIdType.MESH,
        )

    def id_copy(i):
        return pltpu.make_async_remote_copy(
            id_rows.at[me], id_rows.at[me], id_send, id_recv,
            device_id=peer(i), device_id_type=pl.DeviceIdType.MESH,
        )

    def p_copy(i):
        return pltpu.make_async_remote_copy(
            packed.at[me], packed.at[me], p_send, p_recv,
            device_id=peer(i), device_id_type=pl.DeviceIdType.MESH,
        )

    def wait_all(ref, sem):
        part = ref.at[pl.ds(0, total - 1)]
        pltpu.make_async_copy(part, part, sem).wait()

    barrier = pltpu.get_barrier_semaphore()
    each(total - 1, lambda i: pl.semaphore_signal(
        barrier, inc=1, device_id=peer(i), device_id_type=pl.DeviceIdType.MESH))

    for c in range(pieces):
        own_copy(c).start()
    shrink_copy.start()
    for c in range(pieces):
        gate_copy(c).start()
        up_copy(c).start()
    expand_copy.start()

    lane = lax.broadcasted_iota(jnp.int32, (1, rows), 1)
    id_row = jnp.zeros((1, rows), jnp.int32)
    for j in range(row_dev):
        id_row = jnp.where(lax.rem(lane, row_dev) == j, ids[j], id_row)
    id_rows[me] = id_row
    gate_acc[...] = jnp.zeros_like(gate_acc)
    up_acc[...] = jnp.zeros_like(up_acc)
    shrink_acc[...] = jnp.zeros_like(shrink_acc)
    for c in range(pieces):
        own_copy(c).wait()

    pl.semaphore_wait(barrier, total - 1)
    for c in range(pieces):
        each(line - 1, lambda d, c=c: z_copy(c, d).start())
        if c == 0:
            each(total - 1, lambda i: id_copy(i).start())

    wait_all(id_rows, id_recv)
    owner = lax.broadcasted_iota(jnp.int32, (total, 1, rows), 0)
    lane3 = lax.broadcasted_iota(jnp.int32, (total, 1, rows), 2)
    id_row = jnp.sum(jnp.where(lane3 // row_dev == owner, id_rows[...], 0), axis=0)
    across = lax.broadcasted_iota(jnp.int32, (rows, rows), 1)
    down = lax.broadcasted_iota(jnp.int32, (rows, rows), 0)
    id_wide = jnp.broadcast_to(id_row, (rows, rows)).astype(jnp.float32)
    id_col = jnp.sum(jnp.where(across == down, id_wide, 0.0), axis=1, keepdims=True)
    same = jnp.where(id_wide == id_col, 1.0, 0.0)
    slot_col = jnp.sum(jnp.where(across < down, same, 0.0), axis=1, keepdims=True)
    slot_row = jnp.sum(jnp.where(down < across, same, 0.0), axis=0, keepdims=True)
    slots_of[0] = jnp.broadcast_to(id_col, (rows, 128))
    slots_of[1] = jnp.broadcast_to(slot_col, (rows, 128))
    mine = id_row.astype(jnp.float32) == me.astype(jnp.float32)
    slot_id = lax.broadcasted_iota(jnp.int32, (half, rows), 0).astype(jnp.float32)
    pick_low = jnp.where(mine & (slot_row == slot_id), 1.0, 0.0).astype(jnp.bfloat16)
    pick_high = jnp.where(mine & (slot_row == slot_id + half), 1.0, 0.0).astype(jnp.bfloat16)

    def multiply(c):
        gate_copy(c).wait()
        up_copy(c).wait()
        where = pl.ds(pl.multiple_of(c * depth, depth), depth)
        piece = left[c]
        gate_acc[...] += jnp.dot(piece, gate_in[where], preferred_element_type=jnp.float32)
        up_acc[...] += jnp.dot(piece, up_in[where], preferred_element_type=jnp.float32)

    shrink_copy.wait()

    @pl.loop(0, pieces + 2)
    def _(s):
        @pl.when(s < pieces)
        def _():
            each(line - 1, lambda d: z_copy(s, d).wait_recv())
            if pairs > 1:
                y_copy(s).start()

        @pl.when((s >= 1) & (s < pieces + 1))
        def _():
            c = s - 1
            if pairs > 1:
                y_copy(c).wait_recv()
            c_copy(c).start()

        @pl.when(s >= 2)
        def _():
            c = s - 2
            c_copy(c).wait_recv()
            blocks = [
                rows_in[c, kk, yy, zz].astype(jnp.float32)
                for zz in range(line) for yy in range(pairs) for kk in range(CORES)
            ]
            piece = jnp.concatenate(blocks, axis=0).astype(jnp.bfloat16)
            left[c] = piece
            where = pl.ds(pl.multiple_of(c * depth, depth), depth)
            shrink_acc[...] += jnp.dot(piece, shrink_in[where], preferred_element_type=jnp.float32)

        @pl.when(s >= 2 + LAG)
        def _():
            multiply(s - 2 - LAG)

    shrunk = shrink_acc[...]
    shrunk = jnp.concatenate([shrunk, shrunk], axis=1).astype(jnp.bfloat16)
    lane_p = lax.broadcasted_iota(jnp.int32, (half, 2 * rank), 1)
    low = jnp.dot(pick_low, shrunk, preferred_element_type=jnp.float32)
    high = jnp.dot(pick_high, shrunk, preferred_element_type=jnp.float32)
    packed[me] = jnp.where(lane_p < rank, low, high).astype(jnp.bfloat16)
    each(total - 1, lambda i: p_copy(i).start())

    @pl.loop(pieces - LAG, pieces)
    def _(c):
        multiply(c)

    for c in range(pieces):
        each(line - 1, lambda d, c=c: z_copy(c, d).wait_send())
        if pairs > 1:
            y_copy(c).wait_send()
        c_copy(c).wait_send()
    wait_all(id_rows, id_send)

    expand_copy.wait()
    wait_all(packed, p_recv)
    wait_all(packed, p_send)
    id_col = slots_of[0][:, :1]
    slot_col = slots_of[1][:, :1]
    in_high = slot_col >= half
    at = id_col * half + jnp.where(in_high, slot_col - half, slot_col)
    column = lax.broadcasted_iota(jnp.int32, (rows, total * half), 1).astype(jnp.float32)
    pick = jnp.where(column == at, 1.0, 0.0).astype(jnp.bfloat16)
    found = jnp.dot(
        pick, packed[...].reshape(total * half, 2 * rank), preferred_element_type=jnp.float32
    )
    turned = jnp.concatenate([found[:, rank:], found[:, :rank]], axis=1)
    lane_r = lax.broadcasted_iota(jnp.int32, (rows, 2 * rank), 1)
    both = jnp.where((lane_r < rank) != in_high, found, turned)
    second = jnp.where(lane_r < rank, 0.0, 1.0)
    for j in range(adapters // 2):
        wide[:, j * 2 * rank:(j + 1) * 2 * rank] = jnp.where(
            id_col == second + 2.0 * j, both, 0.0).astype(jnp.bfloat16)
    delta = jnp.dot(wide[...], expand_in[...], preferred_element_type=jnp.float32)
    out[...] = (jax.nn.silu(gate_acc[...]) * (up_acc[...] + delta)).astype(jnp.bfloat16)


def local(pairs, tokens, adapter_ids, gate_weight, up_weight, shrink_factors, expand_factors):
    total = lax.axis_size("tensor")
    line = total // (pairs * CORES)
    row_dev, width = tokens.shape
    rows = row_dev * total
    hidden = gate_weight.shape[1]
    adapters, rank, _ = expand_factors.shape
    half = 2 * row_dev
    pieces = 8
    depth = width // pieces
    anywhere = pl.BlockSpec(memory_space=pl.ANY)
    dma = pltpu.SemaphoreType.DMA
    bf16, f32 = jnp.bfloat16, jnp.float32
    return pl.pallas_call(
        functools.partial(step_kernel, line, pairs, pieces),
        out_shape=jax.ShapeDtypeStruct((rows, hidden), bf16),
        in_specs=[anywhere, pl.BlockSpec(memory_space=pltpu.SMEM)] + [anywhere] * 4,
        out_specs=pl.BlockSpec(memory_space=pltpu.VMEM),
        scratch_shapes=[
            pltpu.VMEM((pieces, CORES, pairs, line, row_dev, depth), bf16),
            pltpu.VMEM((width, hidden), bf16),
            pltpu.VMEM((width, hidden), bf16),
            pltpu.VMEM((width, rank), bf16),
            pltpu.VMEM((adapters * rank, hidden), bf16),
            pltpu.VMEM((pieces, rows, depth), bf16),
            pltpu.VMEM((rows, hidden), f32),
            pltpu.VMEM((rows, hidden), f32),
            pltpu.VMEM((rows, rank), f32),
            pltpu.VMEM((total, 1, rows), jnp.int32),
            pltpu.VMEM((total, half, 2 * rank), bf16),
            pltpu.VMEM((2, rows, 128), f32),
            pltpu.VMEM((rows, adapters * rank), bf16),
            dma((pieces,)), dma((pieces,)), dma((pieces,)), dma((2,)),
            dma((pieces, line - 1)), dma((pieces, line - 1)),
            dma((pieces,)), dma((pieces,)), dma((pieces,)), dma((pieces,)),
            dma, dma, dma, dma,
        ],
        compiler_params=pltpu.CompilerParams(
            collective_id=0, has_side_effects=True, vmem_limit_bytes=58 * 2**20
        ),
        cost_estimate=pl.CostEstimate(
            flops=4 * rows * width * hidden,
            bytes_accessed=4 * width * hidden,
            transcendentals=rows * hidden,
        ),
    )(
        tokens, adapter_ids, gate_weight, up_weight,
        shrink_factors.reshape(width, rank), expand_factors.reshape(adapters * rank, hidden),
    )


def solution(mesh):
    pairs = 2 if mesh.shape["tensor"] == 16 else 1
    return jax.shard_map(
        functools.partial(local, pairs),
        mesh=mesh,
        in_specs=(
            P(("groups", "tensor"), None),
            P(("groups", "tensor")),
            P(None, "tensor"),
            P(None, "tensor"),
            P("tensor", None, None),
            P(None, None, "tensor"),
        ),
        out_specs=P("groups", "tensor"),
        check_vma=False,
    )
```

```python
import functools

import jax
import jax.numpy as jnp
from jax import lax
from jax.experimental import pallas as pl
from jax.experimental.pallas import tpu as pltpu
from jax.sharding import PartitionSpec as P

CORES = 2
SKEW = 2
LAG = 6
EARLY = 2
ID_STEP = 3
AHEAD = 3


def each(count, body):
    if count <= 4:
        for i in range(count):
            body(i)
    else:
        lax.fori_loop(0, count, lambda i, carry: (body(i), carry)[1], 0)


def step_kernel(
    line, pairs, pieces,
    tokens, ids, gate_weight, up_weight, shrink, expand,
    out,
    rows_in, gate_in, up_in, shrink_in, expand_in, left, gate_acc, up_acc, shrink_acc,
    id_rows, packed, slots_of, picks, wide,
    own_sem, gate_sem, up_sem, small_sem, z_send, z_recv, y_send, y_recv, c_send, c_recv,
    id_send, id_recv, p_send, p_recv,
):
    total = line * pairs * CORES
    row_dev = tokens.shape[0]
    rows = total * row_dev
    depth = tokens.shape[1] // pieces
    rank = shrink.shape[0]
    half = packed.shape[1]
    adapters = expand.shape[0] // rank

    me = lax.axis_index("tensor")
    k = lax.rem(me, CORES)
    y = lax.rem(me // CORES, pairs)
    z = me // (CORES * pairs)

    def place(zz, yy, kk):
        return {"tensor": (zz * pairs + yy) * CORES + kk}

    def peer(i):
        return {"tensor": lax.rem(me + 1 + i, total)}

    def own_copy(c):
        return pltpu.make_async_copy(
            tokens.at[:, pl.ds(c * depth, depth)], rows_in.at[c, k, y, z], own_sem.at[c]
        )

    def gate_copy(c):
        where = pl.ds(pl.multiple_of(c * depth, depth), depth)
        return pltpu.make_async_copy(gate_weight.at[where], gate_in.at[where], gate_sem.at[c])

    def up_copy(c):
        where = pl.ds(pl.multiple_of(c * depth, depth), depth)
        return pltpu.make_async_copy(up_weight.at[where], up_in.at[where], up_sem.at[c])

    shrink_copy = pltpu.make_async_copy(shrink, shrink_in, small_sem.at[0])
    expand_copy = pltpu.make_async_copy(expand, expand_in, small_sem.at[1])

    def z_copy(c, d):
        block = rows_in.at[c, k, y, z]
        return pltpu.make_async_remote_copy(
            block, block, z_send.at[c, d], z_recv.at[c, d],
            device_id=place(lax.rem(z + d + 1, line), y, k), device_id_type=pl.DeviceIdType.MESH,
        )

    def y_copy(c):
        block = rows_in.at[c, k, y]
        return pltpu.make_async_remote_copy(
            block, block, y_send.at[c], y_recv.at[c],
            device_id=place(z, 1 - y, k), device_id_type=pl.DeviceIdType.MESH,
        )

    def c_copy(c):
        block = rows_in.at[c, k]
        return pltpu.make_async_remote_copy(
            block, block, c_send.at[c], c_recv.at[c],
            device_id=place(z, y, 1 - k), device_id_type=pl.DeviceIdType.MESH,
        )

    def id_copy(i):
        return pltpu.make_async_remote_copy(
            id_rows.at[me], id_rows.at[me], id_send, id_recv,
            device_id=peer(i), device_id_type=pl.DeviceIdType.MESH,
        )

    def p_copy(i):
        return pltpu.make_async_remote_copy(
            packed.at[me], packed.at[me], p_send, p_recv,
            device_id=peer(i), device_id_type=pl.DeviceIdType.MESH,
        )

    def wait_all(ref, sem):
        part = ref.at[pl.ds(0, total - 1)]
        pltpu.make_async_copy(part, part, sem).wait()

    barrier = pltpu.get_barrier_semaphore()
    each(total - 1, lambda i: pl.semaphore_signal(
        barrier, inc=1, device_id=peer(i), device_id_type=pl.DeviceIdType.MESH))

    for c in range(pieces):
        own_copy(c).start()
    shrink_copy.start()
    for c in range(EARLY):
        gate_copy(c).start()
        up_copy(c).start()

    lane = lax.broadcasted_iota(jnp.int32, (1, rows), 1)
    id_row = jnp.zeros((1, rows), jnp.int32)
    for j in range(row_dev):
        id_row = jnp.where(lax.rem(lane, row_dev) == j, ids[j], id_row)
    id_rows[me] = id_row
    gate_acc[...] = jnp.zeros_like(gate_acc)
    up_acc[...] = jnp.zeros_like(up_acc)
    shrink_acc[...] = jnp.zeros_like(shrink_acc)
    for c in range(pieces):
        own_copy(c).wait()

    pl.semaphore_wait(barrier, total - 1)
    for c in range(AHEAD):
        each(line - 1, lambda d, c=c: z_copy(c, d).start())
        if c == 0:
            each(total - 1, lambda i: id_copy(i).start())

    def place_rows():
        wait_all(id_rows, id_recv)
        owner = lax.broadcasted_iota(jnp.int32, (total, 1, rows), 0)
        lane3 = lax.broadcasted_iota(jnp.int32, (total, 1, rows), 2)
        id_row = jnp.sum(jnp.where(lane3 // row_dev == owner, id_rows[...], 0), axis=0)
        across = lax.broadcasted_iota(jnp.int32, (rows, rows), 1)
        down = lax.broadcasted_iota(jnp.int32, (rows, rows), 0)
        id_wide = jnp.broadcast_to(id_row, (rows, rows)).astype(jnp.float32)
        id_col = jnp.sum(jnp.where(across == down, id_wide, 0.0), axis=1, keepdims=True)
        same = jnp.where(id_wide == id_col, 1.0, 0.0)
        slot_col = jnp.sum(jnp.where(across < down, same, 0.0), axis=1, keepdims=True)
        slot_row = jnp.sum(jnp.where(down < across, same, 0.0), axis=0, keepdims=True)
        slots_of[0] = jnp.broadcast_to(id_col, (rows, 128))
        slots_of[1] = jnp.broadcast_to(slot_col, (rows, 128))
        mine = id_row.astype(jnp.float32) == me.astype(jnp.float32)
        slot_id = lax.broadcasted_iota(jnp.int32, (half, rows), 0).astype(jnp.float32)
        picks[0] = jnp.where(mine & (slot_row == slot_id), 1.0, 0.0).astype(jnp.bfloat16)
        picks[1] = jnp.where(mine & (slot_row == slot_id + half), 1.0, 0.0).astype(jnp.bfloat16)

    def multiply(c):
        gate_copy(c).wait()
        up_copy(c).wait()
        where = pl.ds(pl.multiple_of(c * depth, depth), depth)
        piece = left[c]
        gate_acc[...] += jnp.dot(piece, gate_in[where], preferred_element_type=jnp.float32)
        up_acc[...] += jnp.dot(piece, up_in[where], preferred_element_type=jnp.float32)

    shrink_copy.wait()

    @pl.loop(0, pieces + 2 * SKEW)
    def _(s):
        @pl.when(s < pieces)
        def _():
            each(line - 1, lambda d: z_copy(s, d).wait_recv())
            if pairs > 1:
                y_copy(s).start()

        @pl.when(s + AHEAD < pieces)
        def _():
            each(line - 1, lambda d: z_copy(s + AHEAD, d).start())

        @pl.when(s + EARLY < pieces)
        def _():
            gate_copy(s + EARLY).start()
            up_copy(s + EARLY).start()

        @pl.when(s == pieces - EARLY)
        def _():
            expand_copy.start()

        @pl.when((s >= SKEW) & (s < pieces + SKEW))
        def _():
            c = s - SKEW
            if pairs > 1:
                y_copy(c).wait_recv()
            c_copy(c).start()

        @pl.when(s == ID_STEP)
        def _():
            place_rows()

        @pl.when(s >= 2 * SKEW)
        def _():
            c = s - 2 * SKEW
            c_copy(c).wait_recv()
            blocks = [
                rows_in[c, kk, yy, zz].astype(jnp.float32)
                for zz in range(line) for yy in range(pairs) for kk in range(CORES)
            ]
            piece = jnp.concatenate(blocks, axis=0).astype(jnp.bfloat16)
            left[c] = piece
            where = pl.ds(pl.multiple_of(c * depth, depth), depth)
            shrink_acc[...] += lax.dot_general(
                piece, shrink_in[:, where], (((1,), (1,)), ((), ())),
                preferred_element_type=jnp.float32,
            )

        @pl.when(s >= 2 * SKEW + LAG)
        def _():
            multiply(s - 2 * SKEW - LAG)

    shrunk = shrink_acc[...]
    shrunk = jnp.concatenate([shrunk, shrunk], axis=1).astype(jnp.bfloat16)
    lane_p = lax.broadcasted_iota(jnp.int32, (half, 2 * rank), 1)
    low = jnp.dot(picks[0], shrunk, preferred_element_type=jnp.float32)
    high = jnp.dot(picks[1], shrunk, preferred_element_type=jnp.float32)
    packed[me] = jnp.where(lane_p < rank, low, high).astype(jnp.bfloat16)
    each(total - 1, lambda i: p_copy(i).start())

    @pl.loop(pieces - LAG, pieces)
    def _(c):
        multiply(c)

    for c in range(pieces):
        each(line - 1, lambda d, c=c: z_copy(c, d).wait_send())
        if pairs > 1:
            y_copy(c).wait_send()
        c_copy(c).wait_send()
    wait_all(id_rows, id_send)

    expand_copy.wait()
    wait_all(packed, p_recv)
    wait_all(packed, p_send)
    id_col = slots_of[0][:, :1]
    slot_col = slots_of[1][:, :1]
    in_high = slot_col >= half
    at = id_col * half + jnp.where(in_high, slot_col - half, slot_col)
    column = lax.broadcasted_iota(jnp.int32, (rows, total * half), 1).astype(jnp.float32)
    pick = jnp.where(column == at, 1.0, 0.0).astype(jnp.bfloat16)
    found = jnp.dot(
        pick, packed[...].reshape(total * half, 2 * rank), preferred_element_type=jnp.float32
    )
    turned = jnp.concatenate([found[:, rank:], found[:, :rank]], axis=1)
    lane_r = lax.broadcasted_iota(jnp.int32, (rows, 2 * rank), 1)
    both = jnp.where((lane_r < rank) != in_high, found, turned)
    second = jnp.where(lane_r < rank, 0.0, 1.0)
    for j in range(adapters // 2):
        wide[:, j * 2 * rank:(j + 1) * 2 * rank] = jnp.where(
            id_col == second + 2.0 * j, both, 0.0).astype(jnp.bfloat16)
    delta = jnp.dot(wide[...], expand_in[...], preferred_element_type=jnp.float32)
    out[...] = (jax.nn.silu(gate_acc[...]) * (up_acc[...] + delta)).astype(jnp.bfloat16)


def local(pairs, tokens, adapter_ids, gate_weight, up_weight, shrink_factors, expand_factors):
    total = lax.axis_size("tensor")
    line = total // (pairs * CORES)
    row_dev, width = tokens.shape
    rows = row_dev * total
    hidden = gate_weight.shape[1]
    adapters, rank, _ = expand_factors.shape
    half = 2 * row_dev
    pieces = 8
    depth = width // pieces
    anywhere = pl.BlockSpec(memory_space=pl.ANY)
    dma = pltpu.SemaphoreType.DMA
    bf16, f32 = jnp.bfloat16, jnp.float32
    return pl.pallas_call(
        functools.partial(step_kernel, line, pairs, pieces),
        out_shape=jax.ShapeDtypeStruct((rows, hidden), bf16),
        in_specs=[anywhere, pl.BlockSpec(memory_space=pltpu.SMEM)] + [anywhere] * 4,
        out_specs=pl.BlockSpec(memory_space=pltpu.VMEM),
        scratch_shapes=[
            pltpu.VMEM((pieces, CORES, pairs, line, row_dev, depth), bf16),
            pltpu.VMEM((width, hidden), bf16),
            pltpu.VMEM((width, hidden), bf16),
            pltpu.VMEM((rank, width), bf16),
            pltpu.VMEM((adapters * rank, hidden), bf16),
            pltpu.VMEM((pieces, rows, depth), bf16),
            pltpu.VMEM((rows, hidden), f32),
            pltpu.VMEM((rows, hidden), f32),
            pltpu.VMEM((rows, rank), f32),
            pltpu.VMEM((total, 1, rows), jnp.int32),
            pltpu.VMEM((total, half, 2 * rank), bf16),
            pltpu.VMEM((2, rows, 128), f32),
            pltpu.VMEM((2, half, rows), bf16),
            pltpu.VMEM((rows, adapters * rank), bf16),
            dma((pieces,)), dma((pieces,)), dma((pieces,)), dma((2,)),
            dma((pieces, line - 1)), dma((pieces, line - 1)),
            dma((pieces,)), dma((pieces,)), dma((pieces,)), dma((pieces,)),
            dma, dma, dma, dma,
        ],
        compiler_params=pltpu.CompilerParams(
            collective_id=0, has_side_effects=True, vmem_limit_bytes=58 * 2**20
        ),
        cost_estimate=pl.CostEstimate(
            flops=4 * rows * width * hidden,
            bytes_accessed=4 * width * hidden,
            transcendentals=rows * hidden,
        ),
    )(
        tokens, adapter_ids, gate_weight, up_weight,
        shrink_factors[0].T, expand_factors.reshape(adapters * rank, hidden),
    )


def solution(mesh):
    pairs = 2 if mesh.shape["tensor"] == 16 else 1
    return jax.shard_map(
        functools.partial(local, pairs),
        mesh=mesh,
        in_specs=(
            P(("groups", "tensor"), None),
            P(("groups", "tensor")),
            P(None, "tensor"),
            P(None, "tensor"),
            P("tensor", None, None),
            P(None, None, "tensor"),
        ),
        out_specs=P("groups", "tensor"),
        check_vma=False,
    )
```

```python
import functools

import jax
import jax.numpy as jnp
from jax import lax
from jax.experimental import pallas as pl
from jax.experimental.pallas import tpu as pltpu
from jax.sharding import PartitionSpec as P

CORES = 2
SKEW = 1
LAG = 4
EARLY = 1
ID_STEP = 4
AHEAD = 3


def each(count, body):
    if count <= 4:
        for i in range(count):
            body(i)
    else:
        lax.fori_loop(0, count, lambda i, carry: (body(i), carry)[1], 0)


def step_kernel(
    line, pairs, pieces,
    tokens, ids, gate_weight, up_weight, shrink, expand,
    out,
    rows_in, gate_in, up_in, shrink_in, expand_in, left, gate_acc, up_acc, shrink_acc,
    id_rows, packed, slots_of, picks, wide,
    own_sem, gate_sem, up_sem, small_sem, z_send, z_recv, y_send, y_recv, c_send, c_recv,
    id_send, id_recv, p_send, p_recv,
):
    total = line * pairs * CORES
    row_dev = tokens.shape[0]
    rows = total * row_dev
    depth = tokens.shape[1] // pieces
    rank = shrink.shape[0]
    half = packed.shape[1]
    adapters = expand.shape[0] // rank

    me = lax.axis_index("tensor")
    k = lax.rem(me, CORES)
    y = lax.rem(me // CORES, pairs)
    z = me // (CORES * pairs)

    def place(zz, yy, kk):
        return {"tensor": (zz * pairs + yy) * CORES + kk}

    def peer(i):
        return {"tensor": lax.rem(me + 1 + i, total)}

    def own_copy(c):
        return pltpu.make_async_copy(
            tokens.at[:, pl.ds(c * depth, depth)], rows_in.at[c, k, y, 0], own_sem.at[c]
        )

    def gate_copy(c):
        where = pl.ds(pl.multiple_of(c * depth, depth), depth)
        return pltpu.make_async_copy(gate_weight.at[where], gate_in.at[where], gate_sem.at[c])

    def up_copy(c):
        where = pl.ds(pl.multiple_of(c * depth, depth), depth)
        return pltpu.make_async_copy(up_weight.at[where], up_in.at[where], up_sem.at[c])

    shrink_copy = pltpu.make_async_copy(shrink, shrink_in, small_sem.at[0])
    expand_copy = pltpu.make_async_copy(expand, expand_in, small_sem.at[1])

    def z_copy(c, d):
        return pltpu.make_async_remote_copy(
            rows_in.at[c, k, y, 0], rows_in.at[c, k, y, line - 1 - d], z_send.at[c, d], z_recv.at[c, d],
            device_id=place(lax.rem(z + d + 1, line), y, k), device_id_type=pl.DeviceIdType.MESH,
        )

    def y_own(c):
        block = rows_in.at[c, k, y, 0]
        return pltpu.make_async_remote_copy(
            block, block, y_send.at[0, c], y_recv.at[0, c],
            device_id=place(z, 1 - y, k), device_id_type=pl.DeviceIdType.MESH,
        )

    def y_copy(c):
        block = rows_in.at[c, k, y, pl.ds(1, line - 1)]
        return pltpu.make_async_remote_copy(
            block, block, y_send.at[1, c], y_recv.at[1, c],
            device_id=place(z, 1 - y, k), device_id_type=pl.DeviceIdType.MESH,
        )

    def c_copy(c):
        block = rows_in.at[c, k]
        return pltpu.make_async_remote_copy(
            block, block, c_send.at[c], c_recv.at[c],
            device_id=place(z, y, 1 - k), device_id_type=pl.DeviceIdType.MESH,
        )

    def id_copy(i):
        return pltpu.make_async_remote_copy(
            id_rows.at[me], id_rows.at[me], id_send, id_recv,
            device_id=peer(i), device_id_type=pl.DeviceIdType.MESH,
        )

    def p_copy(i):
        return pltpu.make_async_remote_copy(
            packed.at[me], packed.at[me], p_send, p_recv,
            device_id=peer(i), device_id_type=pl.DeviceIdType.MESH,
        )

    def wait_all(ref, sem):
        part = ref.at[pl.ds(0, total - 1)]
        pltpu.make_async_copy(part, part, sem).wait()

    barrier = pltpu.get_barrier_semaphore()
    each(total - 1, lambda i: pl.semaphore_signal(
        barrier, inc=1, device_id=peer(i), device_id_type=pl.DeviceIdType.MESH))

    for c in range(pieces):
        own_copy(c).start()
    shrink_copy.start()
    for c in range(EARLY):
        gate_copy(c).start()
        up_copy(c).start()

    lane = lax.broadcasted_iota(jnp.int32, (1, rows), 1)
    id_row = jnp.zeros((1, rows), jnp.int32)
    for j in range(row_dev):
        id_row = jnp.where(lax.rem(lane, row_dev) == j, ids[j], id_row)
    id_rows[me] = id_row
    gate_acc[...] = jnp.zeros_like(gate_acc)
    up_acc[...] = jnp.zeros_like(up_acc)
    shrink_acc[...] = jnp.zeros_like(shrink_acc)
    for c in range(pieces):
        own_copy(c).wait()

    pl.semaphore_wait(barrier, total - 1)
    for c in range(AHEAD):
        each(line - 1, lambda d, c=c: z_copy(c, d).start())
    if pairs > 1:
        for c in range(pieces):
            y_own(c).start()
    each(total - 1, lambda i: id_copy(i).start())

    def place_rows():
        wait_all(id_rows, id_recv)
        owner = lax.broadcasted_iota(jnp.int32, (total, 1, rows), 0)
        lane3 = lax.broadcasted_iota(jnp.int32, (total, 1, rows), 2)
        id_row = jnp.sum(jnp.where(lane3 // row_dev == owner, id_rows[...], 0), axis=0)
        across = lax.broadcasted_iota(jnp.int32, (rows, rows), 1)
        down = lax.broadcasted_iota(jnp.int32, (rows, rows), 0)
        id_wide = jnp.broadcast_to(id_row, (rows, rows)).astype(jnp.float32)
        id_col = jnp.sum(jnp.where(across == down, id_wide, 0.0), axis=1, keepdims=True)
        same = jnp.where(id_wide == id_col, 1.0, 0.0)
        slot_col = jnp.sum(jnp.where(across < down, same, 0.0), axis=1, keepdims=True)
        slot_row = jnp.sum(jnp.where(down < across, same, 0.0), axis=0, keepdims=True)
        slots_of[0] = jnp.broadcast_to(id_col, (rows, 128))
        slots_of[1] = jnp.broadcast_to(slot_col, (rows, 128))
        mine = id_row.astype(jnp.float32) == me.astype(jnp.float32)
        slot_id = lax.broadcasted_iota(jnp.int32, (half, rows), 0).astype(jnp.float32)
        picks[0] = jnp.where(mine & (slot_row == slot_id), 1.0, 0.0).astype(jnp.bfloat16)
        picks[1] = jnp.where(mine & (slot_row == slot_id + half), 1.0, 0.0).astype(jnp.bfloat16)

    def multiply(c):
        gate_copy(c).wait()
        up_copy(c).wait()
        where = pl.ds(pl.multiple_of(c * depth, depth), depth)
        piece = left[c]
        gate_acc[...] += jnp.dot(piece, gate_in[where], preferred_element_type=jnp.float32)
        up_acc[...] += jnp.dot(piece, up_in[where], preferred_element_type=jnp.float32)

    shrink_copy.wait()

    @pl.loop(0, pieces + 2 * SKEW)
    def _(s):
        @pl.when(s < pieces)
        def _():
            each(line - 1, lambda d: z_copy(s, d).wait_recv())
            if pairs > 1:
                y_copy(s).start()

        @pl.when(s + AHEAD < pieces)
        def _():
            each(line - 1, lambda d: z_copy(s + AHEAD, d).start())

        @pl.when(s + EARLY < pieces)
        def _():
            gate_copy(s + EARLY).start()
            up_copy(s + EARLY).start()

        @pl.when(s == pieces - EARLY)
        def _():
            expand_copy.start()

        @pl.when((s >= SKEW) & (s < pieces + SKEW))
        def _():
            c = s - SKEW
            if pairs > 1:
                y_own(c).wait_recv()
                y_copy(c).wait_recv()
            c_copy(c).start()

        @pl.when(s == ID_STEP)
        def _():
            place_rows()

        @pl.when(s >= 2 * SKEW)
        def _():
            c = s - 2 * SKEW
            c_copy(c).wait_recv()
            blocks = [
                rows_in[c, kk, yy, lax.rem(zz - z + line, line)].astype(jnp.float32)
                for zz in range(line) for yy in range(pairs) for kk in range(CORES)
            ]
            piece = jnp.concatenate(blocks, axis=0).astype(jnp.bfloat16)
            left[c] = piece
            where = pl.ds(pl.multiple_of(c * depth, depth), depth)
            shrink_acc[...] += lax.dot_general(
                piece, shrink_in[:, where], (((1,), (1,)), ((), ())),
                preferred_element_type=jnp.float32,
            )

        @pl.when(s >= 2 * SKEW + LAG)
        def _():
            multiply(s - 2 * SKEW - LAG)

    shrunk = shrink_acc[...]
    shrunk = jnp.concatenate([shrunk, shrunk], axis=1).astype(jnp.bfloat16)
    lane_p = lax.broadcasted_iota(jnp.int32, (half, 2 * rank), 1)
    low = jnp.dot(picks[0], shrunk, preferred_element_type=jnp.float32)
    high = jnp.dot(picks[1], shrunk, preferred_element_type=jnp.float32)
    packed[me] = jnp.where(lane_p < rank, low, high).astype(jnp.bfloat16)
    each(total - 1, lambda i: p_copy(i).start())

    @pl.loop(pieces - LAG, pieces)
    def _(c):
        multiply(c)

    for c in range(pieces):
        each(line - 1, lambda d, c=c: z_copy(c, d).wait_send())
        if pairs > 1:
            y_own(c).wait_send()
            y_copy(c).wait_send()
        c_copy(c).wait_send()
    wait_all(id_rows, id_send)

    expand_copy.wait()
    wait_all(packed, p_recv)
    wait_all(packed, p_send)
    id_col = slots_of[0][:, :1]
    slot_col = slots_of[1][:, :1]
    in_high = slot_col >= half
    at = id_col * half + jnp.where(in_high, slot_col - half, slot_col)
    column = lax.broadcasted_iota(jnp.int32, (rows, total * half), 1).astype(jnp.float32)
    pick = jnp.where(column == at, 1.0, 0.0).astype(jnp.bfloat16)
    found = jnp.dot(
        pick, packed[...].reshape(total * half, 2 * rank), preferred_element_type=jnp.float32
    )
    turned = jnp.concatenate([found[:, rank:], found[:, :rank]], axis=1)
    lane_r = lax.broadcasted_iota(jnp.int32, (rows, 2 * rank), 1)
    both = jnp.where((lane_r < rank) != in_high, found, turned)
    second = jnp.where(lane_r < rank, 0.0, 1.0)
    for j in range(adapters // 2):
        wide[:, j * 2 * rank:(j + 1) * 2 * rank] = jnp.where(
            id_col == second + 2.0 * j, both, 0.0).astype(jnp.bfloat16)
    delta = jnp.dot(wide[...], expand_in[...], preferred_element_type=jnp.float32)
    out[...] = (jax.nn.silu(gate_acc[...]) * (up_acc[...] + delta)).astype(jnp.bfloat16)


def local(pairs, tokens, adapter_ids, gate_weight, up_weight, shrink_factors, expand_factors):
    total = lax.axis_size("tensor")
    line = total // (pairs * CORES)
    row_dev, width = tokens.shape
    rows = row_dev * total
    hidden = gate_weight.shape[1]
    adapters, rank, _ = expand_factors.shape
    half = 2 * row_dev
    pieces = 4
    depth = width // pieces
    anywhere = pl.BlockSpec(memory_space=pl.ANY)
    dma = pltpu.SemaphoreType.DMA
    bf16, f32 = jnp.bfloat16, jnp.float32
    return pl.pallas_call(
        functools.partial(step_kernel, line, pairs, pieces),
        out_shape=jax.ShapeDtypeStruct((rows, hidden), bf16),
        in_specs=[anywhere, pl.BlockSpec(memory_space=pltpu.SMEM)] + [anywhere] * 4,
        out_specs=pl.BlockSpec(memory_space=pltpu.VMEM),
        scratch_shapes=[
            pltpu.VMEM((pieces, CORES, pairs, line, row_dev, depth), bf16),
            pltpu.VMEM((width, hidden), bf16),
            pltpu.VMEM((width, hidden), bf16),
            pltpu.VMEM((rank, width), bf16),
            pltpu.VMEM((adapters * rank, hidden), bf16),
            pltpu.VMEM((pieces, rows, depth), bf16),
            pltpu.VMEM((rows, hidden), f32),
            pltpu.VMEM((rows, hidden), f32),
            pltpu.VMEM((rows, rank), f32),
            pltpu.VMEM((total, 1, rows), jnp.int32),
            pltpu.VMEM((total, half, 2 * rank), bf16),
            pltpu.VMEM((2, rows, 128), f32),
            pltpu.VMEM((2, half, rows), bf16),
            pltpu.VMEM((rows, adapters * rank), bf16),
            dma((pieces,)), dma((pieces,)), dma((pieces,)), dma((2,)),
            dma((pieces, line - 1)), dma((pieces, line - 1)),
            dma((2, pieces)), dma((2, pieces)), dma((pieces,)), dma((pieces,)),
            dma, dma, dma, dma,
        ],
        compiler_params=pltpu.CompilerParams(
            collective_id=0, has_side_effects=True, vmem_limit_bytes=58 * 2**20
        ),
        cost_estimate=pl.CostEstimate(
            flops=4 * rows * width * hidden,
            bytes_accessed=4 * width * hidden,
            transcendentals=rows * hidden,
        ),
    )(
        tokens, adapter_ids, gate_weight, up_weight,
        shrink_factors[0].T, expand_factors.reshape(adapters * rank, hidden),
    )


def solution(mesh):
    pairs = 2 if mesh.shape["tensor"] == 16 else 1
    return jax.shard_map(
        functools.partial(local, pairs),
        mesh=mesh,
        in_specs=(
            P(("groups", "tensor"), None),
            P(("groups", "tensor")),
            P(None, "tensor"),
            P(None, "tensor"),
            P("tensor", None, None),
            P(None, None, "tensor"),
        ),
        out_specs=P("groups", "tensor"),
        check_vma=False,
    )
```
